256 devices in a mesh: frame: 32 (over z_hi, y, x), dp: 8 (over z_lo, core).
Axes of the slice: x: 4, y: 4, z: 8 (z_hi: 2, z_lo: 4; z = z_hi * 4 + z_lo), core: 2. Of those that a mesh axis runs over, the one named last changes fastest.
Arguments:
- queries: bfloat16 [16, 64, 32, 2048], P('dp', 'frame'), may hold values from -90 to 90
- keys_saved: bfloat16 [16, 64, 32, 2048], P('dp', 'frame'), may hold values from -6 to 6
- values_saved: bfloat16 [16, 64, 32, 2048], P('dp', 'frame'), may hold values from -6 to 6
- grad_output: bfloat16 [16, 64, 32, 2048], P('dp', 'frame'), may hold values from -6 to 6
- w_out: bfloat16 [2048, 2048], P('frame'), may hold values from -0.125 to 0.125
Outputs:
- grad_queries: bfloat16 [16, 64, 32, 2048], P('dp', 'frame')
- grad_keys: bfloat16 [16, 64, 32, 2048], P('dp', 'frame')
- grad_values: bfloat16 [16, 64, 32, 2048], P('dp', 'frame')
- grad_w_out: float32 [2048, 2048], P(('frame', 'dp'))
The draws below stay inside these ranges and needn't reach their ends.
All inputs are finite; a program needn't handle non-finite values.
Results may differ from the reference program's by a relative error of at most 0.015.
Values may be sent and summed in bfloat16 or wider, within the bound.
A program may use at most 128 MiB of HBM per device.

```python
import jax
import jax.numpy as jnp
from jax import lax

HEADS = 16
HEAD_DIM = 128
D = 2048
PATCHES = 32
FRAMES = 64
CLIPS = 16


def draw_pair(key):
    shape_all = (CLIPS, FRAMES, PATCHES, HEADS, HEAD_DIM)
    base_keys = jax.random.truncated_normal(jax.random.fold_in(key, 11), -4.0, 4.0, shape_all)
    base_queries = jax.random.truncated_normal(jax.random.fold_in(key, 12), -4.0, 4.0, shape_all)
    keys_out = base_keys.at[:, 1].set(base_keys[:, 1])
    queries_out = base_queries
    return (queries_out.reshape(CLIPS, FRAMES, PATCHES, D), keys_out.reshape(CLIPS, FRAMES, PATCHES, D))


def draw_queries(key, part):
    return draw_pair(key)[0].astype(jnp.bfloat16)


def draw_keys_saved(key, part):
    return draw_pair(key)[1].astype(jnp.bfloat16)


def raised(result, stream_key, source, target, shards_of, factor):
    def block_of(dim):
        return (jnp.arange(result.shape[dim]) // (result.shape[dim] // shards_of)).reshape((-1,) + (1,) * (result.ndim - 1 - dim))

    near = jax.random.permutation(stream_key, shards_of)[block_of(target)]
    other_side = (block_of(target) + shards_of // 2) % shards_of
    return jnp.where((block_of(source) == near) | (block_of(source) == other_side), factor * result, result)


def levels(rng, dims, pieces, least, high):
    def one(position, blocks):
        draws = jax.random.uniform(jax.random.fold_in(jax.random.fold_in(rng, 6), position), (blocks,), jnp.float32, least / len(pieces), high / len(pieces))
        return jnp.repeat(jnp.exp(draws), dims[position] // blocks).reshape((-1,) + (1,) * (len(dims) - position - 1))

    level = one(*pieces[0])
    for cut in pieces[1:]:
        level = level * one(*cut)
    return level


def scatter_about(own_key, dims, width, most, pieces=(), kind=jnp.bfloat16):
    drawn = jax.random.normal(own_key, dims, jnp.float32) * width
    if len(pieces) > 0:
        drawn = levels(own_key, dims, pieces, -0.22, 0.18) * drawn
    return jnp.clip(drawn, min=-most, max=most).astype(kind)


def noise_with(rng, extent, scale, most, split, heavy, kind=jnp.bfloat16):
    result = scale * jax.random.normal(rng, extent, jnp.float32)
    if split:
        result = result * levels(rng, extent, split, -0.22, 0.18)
    return jnp.clip(raised(result, jax.random.fold_in(rng, 3), *heavy), -most, most).astype(kind)


def setup_inputs(seed: int = 0) -> dict:
    seeds = jax.random.split(jax.random.key(seed), 6)
    queries = draw_queries(jax.random.fold_in(seeds[5], 71), 0)
    keys_saved = draw_keys_saved(jax.random.fold_in(seeds[5], 71), 0)
    values_saved = scatter_about(seeds[2], (CLIPS, FRAMES, PATCHES, D), 1.0, 6.0, ((0, 8), (1, 32)))
    grad_output = noise_with(seeds[3], (CLIPS, FRAMES, PATCHES, D), 1.0, 6.0, ((0, 8), (1, 32)), (1, 3, 32, 2.75))
    w_out = scatter_about(seeds[4], (D, D), D ** -0.5, 0.125, ((0, 32),))
    return dict(queries=queries, keys_saved=keys_saved, values_saved=values_saved, grad_output=grad_output, w_out=w_out)


def clip_backward(queries, keys_saved, values_saved, grad_output, w_out):
    score_scale = HEAD_DIM ** -0.5
    shape_heads = (FRAMES, PATCHES, HEADS, HEAD_DIM)
    query_f = queries.astype(jnp.float32).reshape(shape_heads)
    key_f = keys_saved.astype(jnp.float32).reshape(shape_heads)
    value_f = values_saved.astype(jnp.float32).reshape(shape_heads)
    scores = jnp.einsum("fphd,gphd->phfg", query_f, key_f) * score_scale
    probs = jax.nn.softmax(scores, axis=-1)
    probs_low = probs.astype(jnp.bfloat16)
    attended = jnp.einsum("phfg,gphd->fphd", probs_low.astype(jnp.float32), value_f)
    attended = attended.astype(jnp.bfloat16).reshape(FRAMES * PATCHES, D)
    grad_flat = grad_output.reshape(FRAMES * PATCHES, D)
    grad_att = jnp.dot(grad_flat, w_out.T, preferred_element_type=jnp.float32).astype(jnp.bfloat16)
    grad_att_f = grad_att.astype(jnp.float32).reshape(shape_heads)
    grad_probs = jnp.einsum("fphd,gphd->phfg", grad_att_f, value_f)
    row_delta = jnp.sum(probs * grad_probs, axis=-1, keepdims=True)
    grad_scores = (probs * (grad_probs - row_delta)).astype(jnp.bfloat16).astype(jnp.float32)
    grad_q = (jnp.einsum("phfg,gphd->fphd", grad_scores, key_f) * score_scale).astype(jnp.bfloat16)
    grad_k = (jnp.einsum("phfg,fphd->gphd", grad_scores, query_f) * score_scale).astype(jnp.bfloat16)
    grad_v = jnp.einsum("phfg,fphd->gphd", probs_low.astype(jnp.float32), grad_att_f).astype(jnp.bfloat16)
    weight_term = jnp.dot(attended.T, grad_flat, preferred_element_type=jnp.float32)
    full_shape = (FRAMES, PATCHES, D)
    return grad_q.reshape(full_shape), grad_k.reshape(full_shape), grad_v.reshape(full_shape), weight_term


def reference(queries, keys_saved, values_saved, grad_output, w_out):
    def step_clip(carry, inputs):
        grad_q, grad_k, grad_v, weight_term = clip_backward(inputs[0], inputs[1], inputs[2], inputs[3], w_out)
        return carry + weight_term, (grad_q, grad_k, grad_v)

    start_sum = jnp.zeros((D, D), jnp.float32)
    total, grads = lax.scan(step_clip, start_sum, (queries, keys_saved, values_saved, grad_output))
    return grads[0], grads[1], grads[2], total
```

```python
import functools

import jax
import jax.numpy as jnp
from jax import lax
from jax.experimental import pallas as pl
from jax.experimental.pallas import tpu as pltpu
from jax.sharding import PartitionSpec as P

F32 = jnp.float32
BF16 = jnp.bfloat16
D = 2048
HEAD_DIM = 128
SCALE = HEAD_DIM ** (-0.5)
Q, K, V, G = 0, 1, 2, 3
NT = (((1,), (1,)), ((), ()))
NN = (((1,), (0,)), ((), ()))
TN = (((0,), (0,)), ((), ()))


def dot(a, b, dims):
    return lax.dot_general(a, b, dims, preferred_element_type=F32)


def coords():
    f = lax.axis_index("frame")
    d = lax.axis_index("dp")
    return f // 16, (f // 4) % 4, f % 4, d // 2, d % 2


def dev(zh, y, x, zl, core):
    return {"frame": zh * 16 + y * 4 + x, "dp": zl * 2 + core}


def kernel(
    q_ref, k_ref, v_ref, g_ref, w_ref,
    oq_ref, ok_ref, ov_ref, ow_ref,
    zin, xs, xg, rx, rg, wg, att, gat, os, ro, zs, g1s, g1r, g2s, g2r, g3s, g3r,
    sA, rA, sW, rW, sB, rB, sR, rR, sD, rD, sG, rG,
):
    zh, y, x, zl, core = coords()
    me = y * 4 + x
    ins = (q_ref, k_ref, v_ref, g_ref)
    outs = (oq_ref, ok_ref, ov_ref)
    mine = pl.ds(pl.multiple_of(zh * 16, 16), 16)
    other = pl.ds(pl.multiple_of((1 - zh) * 16, 16), 16)
    pair = dev(1 - zh, y, x, zl, core)
    sibling = dev(zh, y, x, zl, 1 - core)

    def plane(t):
        return lax.rem(y + t // 4, 4), lax.rem(x + lax.rem(t, 4), 4)

    def zdev(t):
        z = lax.rem(zh * 4 + zl + t, 8)
        return z, dev(z // 4, y, x, lax.rem(z, 4), core)

    def send(src, dst, s, r, to):
        cp = pltpu.make_async_remote_copy(
            src_ref=src, dst_ref=dst, send_sem=s, recv_sem=r, device_id=to
        )
        cp.start()

    def drain(ref, sem):
        pltpu.make_async_copy(ref, ref, sem).wait()

    barrier = pltpu.get_barrier_semaphore()

    @pl.loop(1, 16)
    def _(t):
        ty, tx = plane(t)
        pl.semaphore_signal(barrier, inc=1, device_id=dev(zh, ty, tx, zl, core))

    @pl.loop(1, 8)
    def _(t):
        _, to = zdev(t)
        pl.semaphore_signal(barrier, inc=1, device_id=to)

    pl.semaphore_signal(barrier, inc=1, device_id=sibling)
    pl.semaphore_wait(barrier, 23)

    half = pl.ds(pl.multiple_of(core * 32, 32), 32)
    send(w_ref.at[half], wg.at[zh, x, core], sW.at[0], rW.at[0], pair)
    order = (G, Q, K, V)
    for c in range(2):
        for a in order:
            send(ins[a].at[c, :, other], zin.at[a, c], sA.at[a, c], rA.at[a, c], pair)
    wg[zh, x, core] = w_ref[half]

    def source(r):
        return lax.rem(r // 8, 2) * 32 + lax.rem(r // 4, 2) * 16 + (r // 16) * 4 + lax.rem(r, 4)

    rows = lax.broadcasted_iota(jnp.int32, (64, 64), 0)
    cols = lax.broadcasted_iota(jnp.int32, (64, 64), 1)
    perm = jnp.where(source(rows) == cols, 1.0, 0.0).astype(BF16)
    unperm = jnp.where(source(cols) == rows, 1.0, 0.0).astype(BF16)

    def spread(a, c):
        drain(zin.at[a, c], rA.at[a, c])
        own = ins[a][c, :, mine, :].reshape(32, D)
        far = zin[a, c].reshape(32, D)
        out = dot(perm, jnp.concatenate([own, far], axis=0), NN).astype(BF16)
        if a == G:
            xg[c] = out.reshape(4, 16, D)
            rg[c, me] = xg[c, x]

            @pl.loop(1, 16)
            def _(t):
                ty, tx = plane(t)
                send(xg.at[c, tx], rg.at[c, me], sB.at[a, c], rB.at[a, c], dev(zh, ty, tx, zl, core))
        else:
            for i in range(4):
                for j in range(4):
                    part = out[i * 16:i * 16 + 16]
                    xs[a, c, i * 4 + j] = jnp.concatenate(
                        [part[:, j * 256:j * 256 + 256], part[:, 1024 + j * 256:1280 + j * 256]], axis=1
                    )
            rx[a, c, me] = xs[a, c, x * 4 + y]

            @pl.loop(1, 16)
            def _(t):
                ty, tx = plane(t)
                send(xs.at[a, c, tx * 4 + ty], rx.at[a, c, me], sB.at[a, c], rB.at[a, c], dev(zh, ty, tx, zl, core))

    def w_second():
        drain(wg.at[0, 0, 0], rW.at[0])

        @pl.loop(1, 4)
        def _(t):
            send(wg.at[:, x, core], wg.at[:, x, core], sW.at[1], rW.at[1], dev(zh, y, lax.rem(x + t, 4), zl, core))

    def w_third():
        drain(wg.at[:, pl.ds(0, 3), 0], rW.at[1])
        send(wg.at[:, :, core], wg.at[:, :, core], sW.at[2], rW.at[2], sibling)

    lane = lax.broadcasted_iota(jnp.int32, (256, 256), 1)
    line = lax.broadcasted_iota(jnp.int32, (256, 256), 0)
    same = lax.rem(lane, 4) == lax.rem(line, 4)

    def attend(c):
        drain(rg.at[c, pl.ds(0, 15)], rB.at[G, c])
        go = rg[c].reshape(256, D)
        for h in range(2):
            gat[:, h * 256:h * 256 + 256] = dot(go, wg[h].reshape(256, D), NT).astype(BF16)
        for a in (Q, K, V):
            drain(rx.at[a, c, pl.ds(0, 15)], rB.at[a, c])

        @pl.loop(0, 4)
        def _(h):
            col = pl.ds(pl.multiple_of(h * HEAD_DIM, HEAD_DIM), HEAD_DIM)
            query = rx[Q, c, :, :, col].reshape(256, HEAD_DIM)
            key = rx[K, c, :, :, col].reshape(256, HEAD_DIM)
            value = rx[V, c, :, :, col].reshape(256, HEAD_DIM)
            ga = gat[:, col]
            scores = jnp.where(same, dot(query, key, NT) * SCALE, -1e30)
            e = jnp.exp(scores - jnp.max(scores, axis=1, keepdims=True))
            probs = e * (1.0 / jnp.sum(e, axis=1, keepdims=True))
            low = probs.astype(BF16)
            att[c, :, col] = dot(low, value, NN).astype(BF16)
            gp = dot(ga, value, NT)
            delta = jnp.sum(probs * gp, axis=1, keepdims=True)
            gs = (probs * (gp - delta)).astype(BF16)
            os[Q, c, :, :, col] = (dot(gs, key, NN) * SCALE).astype(BF16).reshape(16, 16, HEAD_DIM)
            os[K, c, :, :, col] = (dot(gs, query, TN) * SCALE).astype(BF16).reshape(16, 16, HEAD_DIM)
            os[V, c, :, :, col] = dot(low, ga, TN).astype(BF16).reshape(16, 16, HEAD_DIM)

        slot = x * 4 + y
        for a in range(3):
            ro[a, c, slot] = os[a, c, me]

            @pl.loop(1, 16)
            def _(t):
                ty, tx = plane(t)
                send(os.at[a, c, ty * 4 + tx], ro.at[a, c, slot], sR.at[a, c], rR.at[a, c], dev(zh, ty, tx, zl, core))

    def give_back(a, c):
        drain(ro.at[a, c, pl.ds(0, 15)], rR.at[a, c])
        parts = []
        for i in range(4):
            row = [ro[a, c, i * 4 + j] for j in range(4)]
            parts.append(
                jnp.concatenate([r[:, :256] for r in row] + [r[:, 256:] for r in row], axis=1)
            )
        out = dot(unperm, jnp.concatenate(parts, axis=0), NN).astype(BF16)
        zs[a, c] = out[32:].reshape(2, 16, D)
        send(zs.at[a, c], outs[a].at[c, :, mine], sD.at[a, c], rD.at[a, c], pair)
        outs[a][c, :, mine, :] = out[:32].reshape(2, 16, D)

    def weight_first():
        @pl.loop(0, 8)
        def _(n):
            col = pl.ds(pl.multiple_of(n * 256, 256), 256)
            go = rg[:, :, :, col].reshape(512, 256)
            part = dot(att[...].reshape(512, 512), go, TN)
            part = part.reshape(8, 4, 2, 8, 256)
            for i in range(2):
                g1s[i, :, :, :, col] = part[:, :, i].reshape(2, 4, 32, 256).astype(BF16)

        send(g1s.at[1 - core], g1r, sG.at[0], rG.at[0], sibling)

    def weight_second():
        drain(g1r, rG.at[0])
        for i in range(4):
            g2s[i] = (g1s[core, :, i].astype(F32) + g1r[:, i].astype(F32)).astype(BF16)
        g2r[x] = g2s[x]

        @pl.loop(1, 4)
        def _(t):
            tx = lax.rem(x + t, 4)
            send(g2s.at[tx], g2r.at[x], sG.at[1], rG.at[1], dev(zh, y, tx, zl, core))

    def weight_third():
        drain(g2r.at[pl.ds(0, 3)], rG.at[1])
        total = (g2r[0].astype(F32) + g2r[1].astype(F32)) + (g2r[2].astype(F32) + g2r[3].astype(F32))
        total = total.reshape(8, 8, D)
        g3s[...] = jnp.concatenate([total[:, :, :1024], total[:, :, 1024:]], axis=1).astype(BF16)
        z0, _ = zdev(0)
        g3r[z0] = g3s[z0]

        @pl.loop(1, 8)
        def _(t):
            z, to = zdev(t)
            send(g3s.at[z], g3r.at[z0], sG.at[2], rG.at[2], to)

    def weight_last():
        drain(g3r.at[pl.ds(0, 7)], rG.at[2])
        total = g3r[0].astype(F32)
        for i in range(1, 8):
            total = total + g3r[i].astype(F32)
        ow_ref[:, :1024] = total[:8]
        ow_ref[:, 1024:] = total[8:]

    w_second()
    spread(G, 0)
    w_third()
    for a in (Q, K, V):
        spread(a, 0)
    drain(wg.at[:, :, 0], rW.at[2])
    attend(0)
    spread(G, 1)
    for a in range(3):
        give_back(a, 0)
    for a in (Q, K, V):
        spread(a, 1)
    attend(1)
    weight_first()
    for a in range(3):
        give_back(a, 1)
    weight_second()
    weight_third()
    weight_last()

    drain(wg.at[0, 0, 0], sW.at[0])
    drain(wg.at[:, pl.ds(0, 3), 0], sW.at[1])
    drain(wg.at[:, :, 0], sW.at[2])
    for c in range(2):
        for a in (Q, K, V, G):
            drain(zin.at[a, c], sA.at[a, c])
        drain(rg.at[c, pl.ds(0, 15)], sB.at[G, c])
        for a in (Q, K, V):
            drain(rx.at[a, c, pl.ds(0, 15)], sB.at[a, c])
            drain(ro.at[a, c, pl.ds(0, 15)], sR.at[a, c])
            drain(zs.at[a, c], sD.at[a, c])
            drain(zs.at[a, c], rD.at[a, c])
    drain(g1r, sG.at[0])
    drain(g2r.at[pl.ds(0, 3)], sG.at[1])
    drain(g3r.at[pl.ds(0, 7)], sG.at[2])


def on_device(queries, keys_saved, values_saved, grad_output, w_out):
    vmem = pl.BlockSpec(memory_space=pltpu.VMEM)
    dma = pltpu.SemaphoreType.DMA
    whole = jax.ShapeDtypeStruct(queries.shape, BF16)
    return pl.pallas_call(
        kernel,
        name="attention_backward",
        out_shape=(whole, whole, whole, jax.ShapeDtypeStruct((8, D), F32)),
        in_specs=[vmem] * 5,
        out_specs=(vmem,) * 4,
        scratch_shapes=[
            pltpu.VMEM((4, 2, 2, 16, D), BF16),
            pltpu.VMEM((3, 2, 16, 16, 512), BF16),
            pltpu.VMEM((2, 4, 16, D), BF16),
            pltpu.VMEM((3, 2, 16, 16, 512), BF16),
            pltpu.VMEM((2, 16, 16, D), BF16),
            pltpu.VMEM((2, 4, 2, 32, D), BF16),
            pltpu.VMEM((2, 256, 512), BF16),
            pltpu.VMEM((256, 512), BF16),
            pltpu.VMEM((3, 2, 16, 16, 512), BF16),
            pltpu.VMEM((3, 2, 16, 16, 512), BF16),
            pltpu.VMEM((3, 2, 2, 16, D), BF16),
            pltpu.VMEM((2, 2, 4, 32, D), BF16),
            pltpu.VMEM((2, 4, 32, D), BF16),
            pltpu.VMEM((4, 2, 32, D), BF16),
            pltpu.VMEM((4, 2, 32, D), BF16),
            pltpu.VMEM((8, 16, 1024), BF16),
            pltpu.VMEM((8, 16, 1024), BF16),
            dma((4, 2)), dma((4, 2)),
            dma((3,)), dma((3,)),
            dma((4, 2)), dma((4, 2)),
            dma((3, 2)), dma((3, 2)),
            dma((3, 2)), dma((3, 2)),
            dma((3,)), dma((3,)),
        ],
        compiler_params=pltpu.CompilerParams(
            collective_id=0, has_side_effects=True, vmem_limit_bytes=56 * 1024 * 1024
        ),
        cost_estimate=pl.CostEstimate(flops=5 * 10**9, bytes_accessed=4 * 2**20, transcendentals=2**20),
    )(queries, keys_saved, values_saved, grad_output, w_out)


def solution(mesh):
    split = P("dp", "frame", None, None)
    return jax.shard_map(
        on_device,
        mesh=mesh,
        in_specs=(split, split, split, split, P("frame", None)),
        out_specs=(split, split, split, P(("frame", "dp"), None)),
        check_vma=False,
    )
```

```python
import jax
import jax.numpy as jnp
from jax import lax
from jax.experimental import pallas as pl
from jax.experimental.pallas import tpu as pltpu
from jax.sharding import PartitionSpec as P

F32 = jnp.float32
BF16 = jnp.bfloat16
D = 2048
HALF = 1024
HEAD_DIM = 128
SCALE = HEAD_DIM ** (-0.5)
Q, K, V, G = 0, 1, 2, 3
NT = (((1,), (1,)), ((), ()))
NN = (((1,), (0,)), ((), ()))
TN = (((0,), (0,)), ((), ()))
DEPTH = 6


def dot(a, b, dims):
    return lax.dot_general(a, b, dims, preferred_element_type=F32)


def coords():
    f = lax.axis_index("frame")
    d = lax.axis_index("dp")
    return f // 16, (f // 4) % 4, f % 4, d // 2, d % 2


def dev(zh, y, x, zl, core):
    return {"frame": zh * 16 + y * 4 + x, "dp": zl * 2 + core}


def kernel(
    q_hbm, k_hbm, v_hbm, g_hbm, w_hbm,
    oq_ref, ok_ref, ov_ref, ow_ref,
    q_ref, k_ref, v_ref, g_ref, w_ref,
    gin, zin, xg, xqk, xv, rg, rqk, rv, wg, att, att_t, os, ro, zs, g1s, g1r, g2s, g2r, g3s, g3r,
    ssem, rsem, lsem,
):
    zh, y, x, zl, core = coords()
    me = y * 4 + x
    ins = (q_ref, k_ref, v_ref, g_ref)
    outs = (oq_ref, ok_ref, ov_ref)
    mine = pl.ds(pl.multiple_of(zh * 16, 16), 16)
    other = pl.ds(pl.multiple_of((1 - zh) * 16, 16), 16)
    halves = (zh, 1 - zh)

    def cols(h):
        return pl.ds(pl.multiple_of(h * HALF, HALF), HALF)

    pair = dev(1 - zh, y, x, zl, core)
    sibling = dev(zh, y, x, zl, 1 - core)

    def plane(t):
        return lax.rem(y + t // 4, 4), lax.rem(x + lax.rem(t, 4), 4)

    numbers = {}
    flight = {}

    def expect(ref, *key):
        numbers[key] = len(numbers)
        flight["s", key] = ref
        flight["r", key] = ref

    def send(src, dst, to, *key):
        n = numbers[key]
        pltpu.make_async_remote_copy(
            src_ref=src, dst_ref=dst, send_sem=ssem.at[n], recv_sem=rsem.at[n], device_id=to
        ).start()

    def drain(way, *key):
        ref = flight.pop((way, key), None)
        if ref is not None:
            sem = (ssem if way == "s" else rsem).at[numbers[key]]
            pltpu.make_async_copy(ref, ref, sem).wait()

    loads = [
        pltpu.make_async_copy(src, dst, lsem.at[i])
        for i, (src, dst) in enumerate(
            zip((q_hbm, k_hbm, v_hbm, g_hbm, w_hbm), (q_ref, k_ref, v_ref, g_ref, w_ref))
        )
    ]
    for load in loads:
        load.start()

    barrier = pltpu.get_barrier_semaphore()

    @pl.loop(1, 16)
    def _(t):
        ty, tx = plane(t)
        pl.semaphore_signal(barrier, inc=1, device_id=dev(zh, ty, tx, zl, core))

    @pl.loop(1, 8)
    def _(t):
        z = lax.rem(zh * 4 + zl + t, 8)
        pl.semaphore_signal(barrier, inc=1, device_id=dev(z // 4, y, x, lax.rem(z, 4), core))

    pl.semaphore_signal(barrier, inc=1, device_id=sibling)
    pl.semaphore_wait(barrier, 23)
    for load in loads:
        load.wait()

    rows_half = pl.ds(pl.multiple_of(core * 32, 32), 32)
    steps = ((0, 0), (0, 1), (1, 0), (1, 1))
    queue = []
    for c, s in steps:
        if s == 0:
            queue.append((G, c, s))
        queue += [(a, c, s) for a in (Q, K, V)]
        if (c, s) == (0, 0):
            queue.append(None)

    def pump(n=1):
        for item in queue[:n]:
            if item is None:
                expect(wg.at[0, 0, 0], "W", 0)
                send(w_ref.at[rows_half], wg.at[zh, x, core], pair, "W", 0)
            elif item[0] == G:
                c = item[1]
                expect(gin.at[c], "A", *item)
                send(g_ref.at[c, :, other], gin.at[c], pair, "A", *item)
            else:
                a, c, s = item
                expect(zin.at[a, c, s], "A", *item)
                send(ins[a].at[c, :, other, cols(halves[1 - s])], zin.at[a, c, s], pair, "A", *item)
        del queue[:n]

    pump(DEPTH)

    def w_along(s):
        if s == 1:
            drain("r", "W", 0)
            pump()
        h = halves[s]
        expect(wg.at[0, pl.ds(0, 3), 0], "X", s)

        @pl.loop(1, 4)
        def _(t):
            send(wg.at[h, x, core], wg.at[h, x, core], dev(zh, y, lax.rem(x + t, 4), zl, core), "X", s)

    def w_across(s):
        drain("r", "X", s)
        h = halves[s]
        expect(wg.at[0, :, 0], "S", s)
        send(wg.at[h, :, core], wg.at[h, :, core], sibling, "S", s)

    wg[zh, x, core] = w_ref[rows_half]
    w_along(0)

    def source(r):
        return lax.rem(r // 8, 2) * 32 + lax.rem(r // 4, 2) * 16 + (r // 16) * 4 + lax.rem(r, 4)

    rows64 = lax.broadcasted_iota(jnp.int32, (64, 64), 0)
    cols64 = lax.broadcasted_iota(jnp.int32, (64, 64), 1)
    perm = jnp.where(source(rows64) == cols64, 1.0, 0.0).astype(BF16)
    unperm = jnp.where(source(cols64) == rows64, 1.0, 0.0).astype(BF16)

    def to_plane(src, dst, *key):
        @pl.loop(1, 16)
        def _(t):
            ty, tx = plane(t)
            send(src(ty, tx), dst, dev(zh, ty, tx, zl, core), *key)

    def spread_cotangent(c):
        drain("r", "A", G, c, 0)
        pump()
        own = g_ref[c, :, mine, :].reshape(32, D)
        both = jnp.concatenate([own, gin[c].reshape(32, D)], axis=0)
        xg[c] = dot(perm, both, NN).astype(BF16).reshape(4, 16, D)
        expect(rg.at[c, pl.ds(0, 15)], "B", G, c)
        to_plane(lambda ty, tx: xg.at[c, tx], rg.at[c, me], "B", G, c)
        rg[c, me] = xg[c, x]

    def arranged(a, c, s):
        drain("r", "A", a, c, s)
        pump()
        own = ins[a][c, :, mine, cols(halves[s])].reshape(32, HALF)
        both = jnp.concatenate([own, zin[a, c, s].reshape(32, HALF)], axis=0)
        return dot(perm, both, NN).astype(BF16)

    def spread(c, s):
        for a in (Q, K):
            out = arranged(a, c, s)
            for i in range(4):
                for j in range(4):
                    xqk[c, s, i * 4 + j, a] = out[i * 16:i * 16 + 16, j * 256:j * 256 + 256]
        expect(rqk.at[c, s, pl.ds(0, 15)], "B", Q, c, s)
        to_plane(lambda ty, tx: xqk.at[c, s, tx * 4 + ty], rqk.at[c, s, me], "B", Q, c, s)
        rqk[c, s, me] = xqk[c, s, x * 4 + y]
        out = arranged(V, c, s)
        for i in range(4):
            for j in range(4):
                xv[c, s, i * 4 + j] = out[i * 16:i * 16 + 16, j * 256:j * 256 + 256]
        expect(rv.at[c, s, pl.ds(0, 15)], "B", V, c, s)
        to_plane(lambda ty, tx: xv.at[c, s, tx * 4 + ty], rv.at[c, s, me], "B", V, c, s)
        rv[c, s, me] = xv[c, s, x * 4 + y]

    lane = lax.broadcasted_iota(jnp.int32, (256, 256), 1)
    line = lax.broadcasted_iota(jnp.int32, (256, 256), 0)
    same = lax.rem(lane, 4) == lax.rem(line, 4)

    def attend(c, s):
        drain("r", "S", s)
        drain("r", "B", G, c)
        ga_both = dot(rg[c].reshape(256, D), wg[halves[s]].reshape(256, D), NT).astype(BF16)
        drain("r", "B", Q, c, s)
        drain("r", "B", V, c, s)
        for i in range(2):
            col = slice(i * HEAD_DIM, i * HEAD_DIM + HEAD_DIM)
            query = rqk[c, s, :, 0, :, col].reshape(256, HEAD_DIM)
            key = rqk[c, s, :, 1, :, col].reshape(256, HEAD_DIM)
            value = rv[c, s, :, :, col].reshape(256, HEAD_DIM)
            ga = ga_both[:, col]
            scores = jnp.where(same, dot(query, key, NT) * SCALE, -1e30)
            e = jnp.exp(scores - jnp.max(scores, axis=1, keepdims=True))
            probs = e * (1.0 / jnp.sum(e, axis=1, keepdims=True))
            low = probs.astype(BF16)
            att[c, s, :, col] = dot(low, value, NN).astype(BF16)
            gp = dot(ga, value, NT)
            delta = jnp.sum(probs * gp, axis=1, keepdims=True)
            gs = (probs * (gp - delta)).astype(BF16)
            os[c, s, :, Q, :, col] = (dot(gs, key, NN) * SCALE).astype(BF16).reshape(16, 16, HEAD_DIM)
            os[c, s, :, K, :, col] = (dot(gs, query, TN) * SCALE).astype(BF16).reshape(16, 16, HEAD_DIM)
            os[c, s, :, V, :, col] = dot(low, ga, TN).astype(BF16).reshape(16, 16, HEAD_DIM)
        slot = x * 4 + y
        expect(ro.at[c, s, pl.ds(0, 15)], "R", c, s)
        to_plane(lambda ty, tx: os.at[c, s, ty * 4 + tx], ro.at[c, s, slot], "R", c, s)
        ro[c, s, slot] = os[c, s, me]

    def give_back(c, s):
        drain("r", "R", c, s)
        for a in range(3):
            parts = [
                jnp.concatenate([ro[c, s, i * 4 + j, a] for j in range(4)], axis=1) for i in range(4)
            ]
            out = dot(unperm, jnp.concatenate(parts, axis=0), NN).astype(BF16)
            zs[a, c, s] = out[32:].reshape(2, 16, HALF)
            expect(zs.at[a, c, s], "D", a, c, s)
            send(zs.at[a, c, s], outs[a].at[c, :, mine, cols(halves[s])], pair, "D", a, c, s)
            outs[a][c, :, mine, cols(halves[s])] = out[:32].reshape(2, 16, HALF)

    def weight_first(s):
        for c in range(2):
            att_t[:, c * 256:c * 256 + 256] = att[c, s].T

        @pl.loop(0, 8)
        def _(n):
            col = pl.ds(pl.multiple_of(n * 256, 256), 256)
            part = dot(att_t[...], rg[:, :, :, col].reshape(512, 256), NN)
            part = part.reshape(4, 4, 2, 8, 256)
            for i in range(2):
                g1s[s, i, :, :, col] = part[:, :, i].reshape(4, 32, 256).astype(BF16)

        expect(g1r.at[s], "P", 0, s)
        send(g1s.at[s, 1 - core], g1r.at[s], sibling, "P", 0, s)

    def weight_second(s):
        drain("r", "P", 0, s)
        for i in range(4):
            g2s[s, i] = (g1s[s, core, i].astype(F32) + g1r[s, i].astype(F32)).astype(BF16)
        expect(g2r.at[s, pl.ds(0, 3)], "P", 1, s)

        @pl.loop(1, 4)
        def _(t):
            tx = lax.rem(x + t, 4)
            send(g2s.at[s, tx], g2r.at[s, x], dev(zh, y, tx, zl, core), "P", 1, s)

        g2r[s, x] = g2s[s, x]

    def weight_third(s):
        drain("r", "P", 1, s)
        total = (g2r[s, 0].astype(F32) + g2r[s, 1].astype(F32)) + (g2r[s, 2].astype(F32) + g2r[s, 3].astype(F32))
        total = total.reshape(4, 8, D)
        g3s[s] = jnp.concatenate([total[:, :, :HALF], total[:, :, HALF:]], axis=1).astype(BF16)
        z = zh * 4 + zl
        if s == 0:
            g3r[z] = g3s[s, zl]
        expect(g3r.at[pl.ds(0, 3 + s)], "P", 2, s)

        @pl.loop(1 - s, 4)
        def _(t):
            to = lax.rem(zl + t, 4)
            send(g3s.at[s, to], g3r.at[z], dev(halves[s], y, x, to, core), "P", 2, s)

    def weight_last():
        drain("r", "P", 2, 0)
        drain("r", "P", 2, 1)
        total = g3r[0].astype(F32)
        for i in range(1, 8):
            total = total + g3r[i].astype(F32)
        ow_ref[:, :HALF] = total[:8]
        ow_ref[:, HALF:] = total[8:]

    spread_cotangent(0)
    w_across(0)
    spread(0, 0)
    attend(0, 0)
    w_along(1)
    spread(0, 1)
    give_back(0, 0)
    w_across(1)
    spread_cotangent(1)
    attend(0, 1)
    spread(1, 0)
    give_back(0, 1)
    attend(1, 0)
    weight_first(0)
    spread(1, 1)
    give_back(1, 0)
    weight_second(0)
    attend(1, 1)
    weight_first(1)
    weight_third(0)
    weight_second(1)
    give_back(1, 1)
    weight_third(1)
    weight_last()
    for way, key in list(flight):
        drain(way, *key)


def place(*refs):
    sources, targets, sem = refs[:4], refs[4:8], refs[8]
    copies = [pltpu.make_async_copy(a, b, sem.at[i]) for i, (a, b) in enumerate(zip(sources, targets))]
    for copy in copies:
        copy.start()
    for copy in copies:
        copy.wait()


def on_device(queries, keys_saved, values_saved, grad_output, w_out):
    vmem = pl.BlockSpec(memory_space=pltpu.VMEM)
    dma = pltpu.SemaphoreType.DMA
    whole = jax.ShapeDtypeStruct(queries.shape, BF16)

    def buf(*shape):
        return pltpu.VMEM(shape, BF16)

    shapes = (whole, whole, whole, jax.ShapeDtypeStruct((8, D), F32))
    anywhere = pl.BlockSpec(memory_space=pl.ANY)
    results = pl.pallas_call(
        kernel,
        name="attention_backward",
        out_shape=shapes,
        in_specs=[anywhere] * 5,
        out_specs=(vmem,) * 4,
        scratch_shapes=[
            buf(*queries.shape), buf(*queries.shape), buf(*queries.shape), buf(*queries.shape), buf(*w_out.shape),
            buf(2, 2, 16, D),
            buf(3, 2, 2, 2, 16, HALF),
            buf(2, 4, 16, D),
            buf(2, 2, 16, 2, 16, 256),
            buf(2, 2, 16, 16, 256),
            buf(2, 16, 16, D),
            buf(2, 2, 16, 2, 16, 256),
            buf(2, 2, 16, 16, 256),
            buf(2, 4, 2, 32, D),
            buf(2, 2, 256, 256),
            buf(256, 512),
            buf(2, 2, 16, 3, 16, 256),
            buf(2, 2, 16, 3, 16, 256),
            buf(3, 2, 2, 2, 16, HALF),
            buf(2, 2, 4, 32, D),
            buf(2, 4, 32, D),
            buf(2, 4, 32, D),
            buf(2, 4, 32, D),
            buf(2, 4, 16, HALF),
            buf(8, 16, HALF),
            dma((64,)), dma((64,)), dma((5,)),
        ],
        compiler_params=pltpu.CompilerParams(
            collective_id=0, has_side_effects=True, vmem_limit_bytes=56 * 1024 * 1024
        ),
        cost_estimate=pl.CostEstimate(flops=5 * 10**9, bytes_accessed=4 * 2**20, transcendentals=2**20),
    )(queries, keys_saved, values_saved, grad_output, w_out)
    return pl.pallas_call(
        place,
        name="place_results",
        out_shape=shapes,
        in_specs=[vmem] * 4,
        out_specs=(anywhere,) * 4,
        scratch_shapes=[dma((4,))],
        cost_estimate=pl.CostEstimate(flops=0, bytes_accessed=4 * 2**20, transcendentals=0),
    )(*results)


def solution(mesh):
    split = P("dp", "frame", None, None)
    return jax.shard_map(
        on_device,
        mesh=mesh,
        in_specs=(split, split, split, split, P("frame", None)),
        out_specs=(split, split, split, P(("frame", "dp"), None)),
        check_vma=False,
    )
```

```python
import jax
import jax.numpy as jnp
from jax import lax
from jax.experimental import pallas as pl
from jax.experimental.pallas import tpu as pltpu
from jax.sharding import PartitionSpec as P

F32 = jnp.float32
BF16 = jnp.bfloat16
D = 2048
HALF = 1024
HEAD_DIM = 128
SCALE = HEAD_DIM ** (-0.5)
Q, K, V, G = 0, 1, 2, 3
NT = (((1,), (1,)), ((), ()))
NN = (((1,), (0,)), ((), ()))
TN = (((0,), (0,)), ((), ()))
DEPTH = 6


def dot(a, b, dims):
    return lax.dot_general(a, b, dims, preferred_element_type=F32)


def coords():
    f = lax.axis_index("frame")
    d = lax.axis_index("dp")
    return f // 16, (f // 4) % 4, f % 4, d // 2, d % 2


def dev(zh, y, x, zl, core):
    return {"frame": zh * 16 + y * 4 + x, "dp": zl * 2 + core}


def kernel(
    q_hbm, k_hbm, v_hbm, g_hbm, w_hbm,
    oq_ref, ok_ref, ov_ref, ow_ref,
    q_ref, k_ref, v_ref, g_ref, w_ref,
    gin, zin, xg, xqk, xv, rg, rqk, rv, wg, att, att_t, os, ro, zs, g1s, g1r, g2s, g2r, g3s, g3r,
    ssem, rsem, lsem,
):
    zh, y, x, zl, core = coords()
    me = y * 4 + x
    ins = (q_ref, k_ref, v_ref, g_ref)
    outs = (oq_ref, ok_ref, ov_ref)
    mine = pl.ds(pl.multiple_of(zh * 16, 16), 16)
    other = pl.ds(pl.multiple_of((1 - zh) * 16, 16), 16)
    halves = (zh, 1 - zh)

    def cols(h):
        return pl.ds(pl.multiple_of(h * HALF, HALF), HALF)

    pair = dev(1 - zh, y, x, zl, core)
    sibling = dev(zh, y, x, zl, 1 - core)

    def plane(t):
        return lax.rem(y + t // 4, 4), lax.rem(x + lax.rem(t, 4), 4)

    numbers = {}
    flight = {}

    def expect(ref, *key):
        numbers[key] = len(numbers)
        flight["s", key] = ref
        flight["r", key] = ref

    def send(src, dst, to, *key):
        n = numbers[key]
        pltpu.make_async_remote_copy(
            src_ref=src, dst_ref=dst, send_sem=ssem.at[n], recv_sem=rsem.at[n], device_id=to
        ).start()

    def drain(way, *key):
        ref = flight.pop((way, key), None)
        if ref is not None:
            sem = (ssem if way == "s" else rsem).at[numbers[key]]
            pltpu.make_async_copy(ref, ref, sem).wait()

    loads = [
        pltpu.make_async_copy(src, dst, lsem.at[i])
        for i, (src, dst) in enumerate(
            zip((q_hbm, k_hbm, v_hbm, g_hbm, w_hbm), (q_ref, k_ref, v_ref, g_ref, w_ref))
        )
    ]
    for load in loads:
        load.start()

    barrier = pltpu.get_barrier_semaphore()

    @pl.loop(1, 16)
    def _(t):
        ty, tx = plane(t)
        pl.semaphore_signal(barrier, inc=1, device_id=dev(zh, ty, tx, zl, core))

    @pl.loop(1, 8)
    def _(t):
        z = lax.rem(zh * 4 + zl + t, 8)
        pl.semaphore_signal(barrier, inc=1, device_id=dev(z // 4, y, x, lax.rem(z, 4), core))

    pl.semaphore_signal(barrier, inc=1, device_id=sibling)
    pl.semaphore_wait(barrier, 23)
    for load in loads:
        load.wait()

    rows_half = pl.ds(pl.multiple_of(core * 32, 32), 32)
    steps = ((0, 0), (0, 1), (1, 0), (1, 1))
    queue = []
    for c, s in steps:
        if s == 0:
            queue.append((G, c, s))
        queue += [(a, c, s) for a in (Q, K, V)]
        if (c, s) == (0, 0):
            queue.append(None)

    def pump(n=1):
        for item in queue[:n]:
            if item is None:
                expect(wg.at[0, 0, 0], "W", 0)
                send(w_ref.at[rows_half], wg.at[zh, x, core], pair, "W", 0)
            elif item[0] == G:
                c = item[1]
                expect(gin.at[c], "A", *item)
                for i in range(2):
                    for h in range(2):
                        col = slice(h * HALF, h * HALF + HALF)
                        send(g_ref.at[c, i, other, col], gin.at[c, i, :, col], pair, "A", *item)
            else:
                a, c, s = item
                expect(zin.at[a, c, s], "A", *item)
                send(ins[a].at[c, :, other, cols(halves[1 - s])], zin.at[a, c, s], pair, "A", *item)
        del queue[:n]

    pump(DEPTH)

    def w_along(s):
        if s == 1:
            drain("r", "W", 0)
            pump()
        h = halves[s]
        expect(wg.at[0, pl.ds(0, 3), 0], "X", s)

        @pl.loop(1, 4)
        def _(t):
            send(wg.at[h, x, core], wg.at[h, x, core], dev(zh, y, lax.rem(x + t, 4), zl, core), "X", s)

    def w_across(s):
        drain("r", "X", s)
        h = halves[s]
        expect(wg.at[0, :, 0], "S", s)
        send(wg.at[h, :, core], wg.at[h, :, core], sibling, "S", s)

    wg[zh, x, core] = w_ref[rows_half]
    w_along(0)

    def source(r):
        return lax.rem(r // 8, 2) * 32 + lax.rem(r // 4, 2) * 16 + (r // 16) * 4 + lax.rem(r, 4)

    rows64 = lax.broadcasted_iota(jnp.int32, (64, 64), 0)
    cols64 = lax.broadcasted_iota(jnp.int32, (64, 64), 1)
    perm = jnp.where(source(rows64) == cols64, 1.0, 0.0).astype(BF16)
    unperm = jnp.where(source(cols64) == rows64, 1.0, 0.0).astype(BF16)

    def to_plane(src, dst, *key):
        @pl.loop(1, 16)
        def _(t):
            ty, tx = plane(t)
            send(src(ty, tx), dst, dev(zh, ty, tx, zl, core), *key)

    def spread_cotangent(c):
        drain("r", "A", G, c, 0)
        pump()
        own = g_ref[c, :, mine, :].reshape(32, D)
        both = jnp.concatenate([own, gin[c].reshape(32, D)], axis=0)
        xg[c] = dot(perm, both, NN).astype(BF16).reshape(4, 16, D)
        expect(rg.at[c, pl.ds(0, 15)], "B", G, c)
        to_plane(lambda ty, tx: xg.at[c, tx], rg.at[c, me], "B", G, c)
        rg[c, me] = xg[c, x]

    def arranged(a, c, s):
        drain("r", "A", a, c, s)
        pump()
        own = ins[a][c, :, mine, cols(halves[s])].reshape(32, HALF)
        both = jnp.concatenate([own, zin[a, c, s].reshape(32, HALF)], axis=0)
        return dot(perm, both, NN).astype(BF16)

    def spread(c, s):
        for a in (Q, K):
            out = arranged(a, c, s)
            for i in range(4):
                for j in range(4):
                    xqk[c, s, i * 4 + j, a] = out[i * 16:i * 16 + 16, j * 256:j * 256 + 256]
        expect(rqk.at[c, s, pl.ds(0, 15)], "B", Q, c, s)
        to_plane(lambda ty, tx: xqk.at[c, s, tx * 4 + ty], rqk.at[c, s, me], "B", Q, c, s)
        rqk[c, s, me] = xqk[c, s, x * 4 + y]
        out = arranged(V, c, s)
        for i in range(4):
            for j in range(4):
                xv[c, s, i * 4 + j] = out[i * 16:i * 16 + 16, j * 256:j * 256 + 256]
        expect(rv.at[c, s, pl.ds(0, 15)], "B", V, c, s)
        to_plane(lambda ty, tx: xv.at[c, s, tx * 4 + ty], rv.at[c, s, me], "B", V, c, s)
        rv[c, s, me] = xv[c, s, x * 4 + y]

    lane = lax.broadcasted_iota(jnp.int32, (256, 256), 1)
    line = lax.broadcasted_iota(jnp.int32, (256, 256), 0)
    same = lax.rem(lane, 4) == lax.rem(line, 4)

    def attend(c, s):
        drain("r", "S", s)
        drain("r", "B", G, c)
        ga_both = dot(rg[c].reshape(256, D), wg[halves[s]].reshape(256, D), NT).astype(BF16)
        drain("r", "B", Q, c, s)
        drain("r", "B", V, c, s)
        for i in range(2):
            col = slice(i * HEAD_DIM, i * HEAD_DIM + HEAD_DIM)
            query = rqk[c, s, :, 0, :, col].reshape(256, HEAD_DIM)
            key = rqk[c, s, :, 1, :, col].reshape(256, HEAD_DIM)
            value = rv[c, s, :, :, col].reshape(256, HEAD_DIM)
            ga = ga_both[:, col]
            scores = jnp.where(same, dot(query, key, NT) * SCALE, -1e30)
            e = jnp.exp(scores - jnp.max(scores, axis=1, keepdims=True))
            probs = e * (1.0 / jnp.sum(e, axis=1, keepdims=True))
            low = probs.astype(BF16)
            att[c, s, :, col] = dot(low, value, NN).astype(BF16)
            gp = dot(ga, value, NT)
            delta = jnp.sum(probs * gp, axis=1, keepdims=True)
            gs = (probs * (gp - delta)).astype(BF16)
            os[c, s, :, Q, :, col] = (dot(gs, key, NN) * SCALE).astype(BF16).reshape(16, 16, HEAD_DIM)
            os[c, s, :, K, :, col] = (dot(gs, query, TN) * SCALE).astype(BF16).reshape(16, 16, HEAD_DIM)
            os[c, s, :, V, :, col] = dot(low, ga, TN).astype(BF16).reshape(16, 16, HEAD_DIM)
        slot = x * 4 + y
        for a in range(3):
            expect(ro.at[c, s, pl.ds(0, 15), a], "R", c, s, a)
            to_plane(lambda ty, tx: os.at[c, s, ty * 4 + tx, a], ro.at[c, s, slot, a], "R", c, s, a)
        ro[c, s, slot] = os[c, s, me]

    def give_back(c, s):
        for a in range(3):
            drain("r", "R", c, s, a)
            parts = [
                jnp.concatenate([ro[c, s, i * 4 + j, a] for j in range(4)], axis=1) for i in range(4)
            ]
            out = dot(unperm, jnp.concatenate(parts, axis=0), NN).astype(BF16)
            zs[a, c, s] = out[32:].reshape(2, 16, HALF)
            expect(zs.at[a, c, s], "D", a, c, s)
            send(zs.at[a, c, s], outs[a].at[c, :, mine, cols(halves[s])], pair, "D", a, c, s)
            outs[a][c, :, mine, cols(halves[s])] = out[:32].reshape(2, 16, HALF)

    def weight_first(s):
        for c in range(2):
            att_t[:, c * 256:c * 256 + 256] = att[c, s].T

        @pl.loop(0, 8)
        def _(n):
            col = pl.ds(pl.multiple_of(n * 256, 256), 256)
            part = dot(att_t[...], rg[:, :, :, col].reshape(512, 256), NN)
            part = part.reshape(4, 4, 2, 8, 256)
            for i in range(2):
                g1s[s, i, :, :, col] = part[:, :, i].reshape(4, 32, 256).astype(BF16)

        expect(g1r.at[s], "P", 0, s)
        send(g1s.at[s, 1 - core], g1r.at[s], sibling, "P", 0, s)

    def weight_second(s):
        drain("r", "P", 0, s)
        for i in range(4):
            g2s[s, i] = (g1s[s, core, i].astype(F32) + g1r[s, i].astype(F32)).astype(BF16)
        expect(g2r.at[s, pl.ds(0, 3)], "P", 1, s)

        @pl.loop(1, 4)
        def _(t):
            tx = lax.rem(x + t, 4)
            send(g2s.at[s, tx], g2r.at[s, x], dev(zh, y, tx, zl, core), "P", 1, s)

        g2r[s, x] = g2s[s, x]

    def weight_third(s):
        drain("r", "P", 1, s)
        total = (g2r[s, 0].astype(F32) + g2r[s, 1].astype(F32)) + (g2r[s, 2].astype(F32) + g2r[s, 3].astype(F32))
        total = total.reshape(4, 8, D)
        g3s[s] = jnp.concatenate([total[:, :, :HALF], total[:, :, HALF:]], axis=1).astype(BF16)
        z = zh * 4 + zl
        if s == 0:
            g3r[z] = g3s[s, zl]
        expect(g3r.at[pl.ds(0, 3 + s)], "P", 2, s)

        @pl.loop(1 - s, 4)
        def _(t):
            to = lax.rem(zl + t, 4)
            send(g3s.at[s, to], g3r.at[z], dev(halves[s], y, x, to, core), "P", 2, s)

    def weight_last():
        drain("r", "P", 2, 0)
        drain("r", "P", 2, 1)
        total = g3r[0].astype(F32)
        for i in range(1, 8):
            total = total + g3r[i].astype(F32)
        ow_ref[:, :HALF] = total[:8]
        ow_ref[:, HALF:] = total[8:]

    spread_cotangent(0)
    w_across(0)
    spread(0, 0)
    attend(0, 0)
    w_along(1)
    spread(0, 1)
    give_back(0, 0)
    w_across(1)
    spread_cotangent(1)
    attend(0, 1)
    spread(1, 0)
    give_back(0, 1)
    attend(1, 0)
    weight_first(0)
    spread(1, 1)
    give_back(1, 0)
    weight_second(0)
    attend(1, 1)
    weight_first(1)
    weight_third(0)
    weight_second(1)
    give_back(1, 1)
    weight_third(1)
    weight_last()
    for way, key in list(flight):
        drain(way, *key)


def place(*refs):
    sources, targets, sem = refs[:4], refs[4:8], refs[8]
    copies = [pltpu.make_async_copy(a, b, sem.at[i]) for i, (a, b) in enumerate(zip(sources, targets))]
    for copy in copies:
        copy.start()
    for copy in copies:
        copy.wait()


def on_device(queries, keys_saved, values_saved, grad_output, w_out):
    vmem = pl.BlockSpec(memory_space=pltpu.VMEM)
    dma = pltpu.SemaphoreType.DMA
    whole = jax.ShapeDtypeStruct(queries.shape, BF16)

    def buf(*shape):
        return pltpu.VMEM(shape, BF16)

    shapes = (whole, whole, whole, jax.ShapeDtypeStruct((8, D), F32))
    anywhere = pl.BlockSpec(memory_space=pl.ANY)
    results = pl.pallas_call(
        kernel,
        name="attention_backward",
        out_shape=shapes,
        in_specs=[anywhere] * 5,
        out_specs=(vmem,) * 4,
        scratch_shapes=[
            buf(*queries.shape), buf(*queries.shape), buf(*queries.shape), buf(*queries.shape), buf(*w_out.shape),
            buf(2, 2, 16, D),
            buf(3, 2, 2, 2, 16, HALF),
            buf(2, 4, 16, D),
            buf(2, 2, 16, 2, 16, 256),
            buf(2, 2, 16, 16, 256),
            buf(2, 16, 16, D),
            buf(2, 2, 16, 2, 16, 256),
            buf(2, 2, 16, 16, 256),
            buf(2, 4, 2, 32, D),
            buf(2, 2, 256, 256),
            buf(256, 512),
            buf(2, 2, 16, 3, 16, 256),
            buf(2, 2, 16, 3, 16, 256),
            buf(3, 2, 2, 2, 16, HALF),
            buf(2, 2, 4, 32, D),
            buf(2, 4, 32, D),
            buf(2, 4, 32, D),
            buf(2, 4, 32, D),
            buf(2, 4, 16, HALF),
            buf(8, 16, HALF),
            dma((64,)), dma((64,)), dma((5,)),
        ],
        compiler_params=pltpu.CompilerParams(
            collective_id=0, has_side_effects=True, vmem_limit_bytes=56 * 1024 * 1024
        ),
        cost_estimate=pl.CostEstimate(flops=5 * 10**9, bytes_accessed=4 * 2**20, transcendentals=2**20),
    )(queries, keys_saved, values_saved, grad_output, w_out)
    return pl.pallas_call(
        place,
        name="place_results",
        out_shape=shapes,
        in_specs=[vmem] * 4,
        out_specs=(anywhere,) * 4,
        scratch_shapes=[dma((4,))],
        cost_estimate=pl.CostEstimate(flops=0, bytes_accessed=4 * 2**20, transcendentals=0),
    )(*results)


def solution(mesh):
    split = P("dp", "frame", None, None)
    return jax.shard_map(
        on_device,
        mesh=mesh,
        in_specs=(split, split, split, split, P("frame", None)),
        out_specs=(split, split, split, P(("frame", "dp"), None)),
        check_vma=False,
    )
```

```python
import jax
import jax.numpy as jnp
from jax import lax
from jax.experimental import pallas as pl
from jax.experimental.pallas import tpu as pltpu
from jax.sharding import PartitionSpec as P

F32 = jnp.float32
BF16 = jnp.bfloat16
D = 2048
HALF = 1024
HEAD_DIM = 128
SCALE = HEAD_DIM ** (-0.5)
Q, K, V, G = 0, 1, 2, 3
NT = (((1,), (1,)), ((), ()))
NN = (((1,), (0,)), ((), ()))
TN = (((0,), (0,)), ((), ()))
DEPTH = 6


def dot(a, b, dims):
    return lax.dot_general(a, b, dims, preferred_element_type=F32)


def coords():
    f = lax.axis_index("frame")
    d = lax.axis_index("dp")
    return f // 16, (f // 4) % 4, f % 4, d // 2, d % 2


def dev(zh, y, x, zl, core):
    return {"frame": zh * 16 + y * 4 + x, "dp": zl * 2 + core}


def kernel(
    q_hbm, k_hbm, v_hbm, g_hbm, w_hbm,
    oq_ref, ok_ref, ov_ref, ow_ref,
    q_ref, k_ref, v_ref, g_ref, w_ref,
    gin, zin, xg, xqk, xv, rg, rqk, rv, wg, att, att_t, os, ro, zs, zo, g1s, g1r, g2s, g2r, g3s, g3r,
    ssem, rsem, lsem,
):
    zh, y, x, zl, core = coords()
    me = y * 4 + x
    ins = (q_ref, k_ref, v_ref, g_ref)
    outs = (oq_ref, ok_ref, ov_ref)
    mine = pl.ds(pl.multiple_of(zh * 16, 16), 16)
    other = pl.ds(pl.multiple_of((1 - zh) * 16, 16), 16)
    halves = (zh, 1 - zh)

    def cols(h):
        return pl.ds(pl.multiple_of(h * HALF, HALF), HALF)

    pair = dev(1 - zh, y, x, zl, core)
    sibling = dev(zh, y, x, zl, 1 - core)

    def plane(t):
        return lax.rem(y + t // 4, 4), lax.rem(x + lax.rem(t, 4), 4)

    numbers = {}
    flight = {}

    def expect(ref, *key):
        numbers[key] = len(numbers)
        flight["s", key] = ref
        flight["r", key] = ref

    def send(src, dst, to, *key):
        n = numbers[key]
        pltpu.make_async_remote_copy(
            src_ref=src, dst_ref=dst, send_sem=ssem.at[n], recv_sem=rsem.at[n], device_id=to
        ).start()

    def drain(way, *key):
        ref = flight.pop((way, key), None)
        if ref is not None:
            sem = (ssem if way == "s" else rsem).at[numbers[key]]
            pltpu.make_async_copy(ref, ref, sem).wait()

    loads = [
        pltpu.make_async_copy(src, dst, lsem.at[i])
        for i, (src, dst) in enumerate(
            zip((q_hbm, k_hbm, v_hbm, g_hbm, w_hbm), (q_ref, k_ref, v_ref, g_ref, w_ref))
        )
    ]
    for load in loads:
        load.start()

    barrier = pltpu.get_barrier_semaphore()

    @pl.loop(1, 16)
    def _(t):
        ty, tx = plane(t)
        pl.semaphore_signal(barrier, inc=1, device_id=dev(zh, ty, tx, zl, core))

    @pl.loop(1, 8)
    def _(t):
        z = lax.rem(zh * 4 + zl + t, 8)
        pl.semaphore_signal(barrier, inc=1, device_id=dev(z // 4, y, x, lax.rem(z, 4), core))

    pl.semaphore_signal(barrier, inc=1, device_id=sibling)
    pl.semaphore_wait(barrier, 23)
    for load in loads:
        load.wait()

    rows_half = pl.ds(pl.multiple_of(core * 32, 32), 32)
    steps = ((0, 0), (0, 1), (1, 0), (1, 1))
    queue = []
    for c, s in steps:
        if s == 0:
            queue.append((G, c, s))
        queue += [(a, c, s) for a in (Q, K, V)]
        if (c, s) == (0, 0):
            queue.append(None)

    def pump(n=1):
        for item in queue[:n]:
            if item is None:
                expect(wg.at[0, 0, 0], "W", 0)
                send(w_ref.at[rows_half], wg.at[zh, x, core], pair, "W", 0)
            elif item[0] == G:
                c = item[1]
                expect(gin.at[c], "A", *item)
                for i in range(2):
                    for h in range(2):
                        col = slice(h * HALF, h * HALF + HALF)
                        send(g_ref.at[c, i, other, col], gin.at[c, i, :, col], pair, "A", *item)
            else:
                a, c, s = item
                expect(zin.at[a, c, s], "A", *item)
                send(ins[a].at[c, :, other, cols(halves[1 - s])], zin.at[a, c, s], pair, "A", *item)
        del queue[:n]

    pump(DEPTH)

    def w_along(s):
        if s == 1:
            drain("r", "W", 0)
            pump()
        h = halves[s]
        expect(wg.at[0, pl.ds(0, 3), 0], "X", s)

        @pl.loop(1, 4)
        def _(t):
            send(wg.at[h, x, core], wg.at[h, x, core], dev(zh, y, lax.rem(x + t, 4), zl, core), "X", s)

    def w_across(s):
        drain("r", "X", s)
        h = halves[s]
        expect(wg.at[0, :, 0], "S", s)
        send(wg.at[h, :, core], wg.at[h, :, core], sibling, "S", s)

    wg[zh, x, core] = w_ref[rows_half]
    w_along(0)

    def source(r):
        return lax.rem(r // 8, 2) * 32 + lax.rem(r // 4, 2) * 16 + (r // 16) * 4 + lax.rem(r, 4)

    rows64 = lax.broadcasted_iota(jnp.int32, (64, 64), 0)
    cols64 = lax.broadcasted_iota(jnp.int32, (64, 64), 1)
    perm = jnp.where(source(rows64) == cols64, 1.0, 0.0).astype(BF16)
    unperm = jnp.where(source(cols64) == rows64, 1.0, 0.0).astype(BF16)

    def to_plane(src, dst, *key):
        @pl.loop(1, 16)
        def _(t):
            ty, tx = plane(t)
            send(src(ty, tx), dst, dev(zh, ty, tx, zl, core), *key)

    def spread_cotangent(c):
        drain("r", "A", G, c, 0)
        pump()
        own = g_ref[c, :, mine, :].reshape(32, D)
        both = jnp.concatenate([own, gin[c].reshape(32, D)], axis=0)
        xg[c] = dot(perm, both, NN).astype(BF16).reshape(4, 16, D)
        expect(rg.at[c, pl.ds(0, 15)], "B", G, c)
        to_plane(lambda ty, tx: xg.at[c, tx], rg.at[c, me], "B", G, c)
        rg[c, me] = xg[c, x]

    def arranged(a, c, s):
        drain("r", "A", a, c, s)
        pump()
        own = ins[a][c, :, mine, cols(halves[s])].reshape(32, HALF)
        both = jnp.concatenate([own, zin[a, c, s].reshape(32, HALF)], axis=0)
        return dot(perm, both, NN).astype(BF16)

    def spread(c, s):
        for a in (Q, K):
            out = arranged(a, c, s)
            for i in range(4):
                for j in range(4):
                    xqk[c, s, i * 4 + j, a] = out[i * 16:i * 16 + 16, j * 256:j * 256 + 256]
        expect(rqk.at[c, s, pl.ds(0, 15)], "B", Q, c, s)
        to_plane(lambda ty, tx: xqk.at[c, s, tx * 4 + ty], rqk.at[c, s, me], "B", Q, c, s)
        rqk[c, s, me] = xqk[c, s, x * 4 + y]
        out = arranged(V, c, s)
        for i in range(4):
            for j in range(4):
                xv[c, s, i * 4 + j] = out[i * 16:i * 16 + 16, j * 256:j * 256 + 256]
        expect(rv.at[c, s, pl.ds(0, 15)], "B", V, c, s)
        to_plane(lambda ty, tx: xv.at[c, s, tx * 4 + ty], rv.at[c, s, me], "B", V, c, s)
        rv[c, s, me] = xv[c, s, x * 4 + y]

    lane = lax.broadcasted_iota(jnp.int32, (256, 256), 1)
    line = lax.broadcasted_iota(jnp.int32, (256, 256), 0)
    same = lax.rem(lane, 4) == lax.rem(line, 4)

    def attend(c, s):
        drain("r", "S", s)
        drain("r", "B", G, c)
        ga_both = dot(rg[c].reshape(256, D), wg[halves[s]].reshape(256, D), NT).astype(BF16)
        drain("r", "B", Q, c, s)
        drain("r", "B", V, c, s)
        for i in range(2):
            col = slice(i * HEAD_DIM, i * HEAD_DIM + HEAD_DIM)
            query = rqk[c, s, :, 0, :, col].reshape(256, HEAD_DIM)
            key = rqk[c, s, :, 1, :, col].reshape(256, HEAD_DIM)
            value = rv[c, s, :, :, col].reshape(256, HEAD_DIM)
            ga = ga_both[:, col]
            scores = jnp.where(same, dot(query, key, NT) * SCALE, -1e30)
            e = jnp.exp(scores - jnp.max(scores, axis=1, keepdims=True))
            probs = e * (1.0 / jnp.sum(e, axis=1, keepdims=True))
            low = probs.astype(BF16)
            att[c, s, :, col] = dot(low, value, NN).astype(BF16)
            gp = dot(ga, value, NT)
            delta = jnp.sum(probs * gp, axis=1, keepdims=True)
            gs = (probs * (gp - delta)).astype(BF16)
            os[c, s, :, Q, :, col] = (dot(gs, key, NN) * SCALE).astype(BF16).reshape(16, 16, HEAD_DIM)
            os[c, s, :, K, :, col] = (dot(gs, query, TN) * SCALE).astype(BF16).reshape(16, 16, HEAD_DIM)
            os[c, s, :, V, :, col] = dot(low, ga, TN).astype(BF16).reshape(16, 16, HEAD_DIM)
        slot = x * 4 + y
        for a in range(3):
            expect(ro.at[c, s, pl.ds(0, 15), a], "R", c, s, a)
            to_plane(lambda ty, tx: os.at[c, s, ty * 4 + tx, a], ro.at[c, s, slot, a], "R", c, s, a)
        ro[c, s, slot] = os[c, s, me]

    keeps = []

    def give_back(c, s):
        for a in range(3):
            drain("r", "R", c, s, a)
            parts = [
                jnp.concatenate([ro[c, s, i * 4 + j, a] for j in range(4)], axis=1) for i in range(4)
            ]
            out = dot(unperm, jnp.concatenate(parts, axis=0), NN).astype(BF16)
            zs[a, c, s] = out[32:].reshape(2, 16, HALF)
            expect(zs.at[a, c, s], "D", a, c, s)
            send(zs.at[a, c, s], outs[a].at[c, :, mine, cols(halves[s])], pair, "D", a, c, s)
            zo[a, c, s] = out[:32].reshape(2, 16, HALF)
            kept = pltpu.make_async_copy(
                zo.at[a, c, s], outs[a].at[c, :, mine, cols(halves[s])], lsem.at[5 + len(keeps)]
            )
            kept.start()
            keeps.append(kept)

    def weight_first(s):
        for c in range(2):
            att_t[:, c * 256:c * 256 + 256] = att[c, s].T

        @pl.loop(0, 8)
        def _(n):
            col = pl.ds(pl.multiple_of(n * 256, 256), 256)
            part = dot(att_t[...], rg[:, :, :, col].reshape(512, 256), NN)
            part = part.reshape(4, 4, 2, 8, 256)
            for i in range(2):
                g1s[s, i, :, :, col] = part[:, :, i].reshape(4, 32, 256).astype(BF16)

        expect(g1r.at[s], "P", 0, s)
        send(g1s.at[s, 1 - core], g1r.at[s], sibling, "P", 0, s)

    def weight_second(s):
        drain("r", "P", 0, s)
        for i in range(4):
            g2s[s, i] = (g1s[s, core, i].astype(F32) + g1r[s, i].astype(F32)).astype(BF16)
        expect(g2r.at[s, pl.ds(0, 3)], "P", 1, s)

        @pl.loop(1, 4)
        def _(t):
            tx = lax.rem(x + t, 4)
            send(g2s.at[s, tx], g2r.at[s, x], dev(zh, y, tx, zl, core), "P", 1, s)

        g2r[s, x] = g2s[s, x]

    def weight_third(s):
        drain("r", "P", 1, s)
        total = (g2r[s, 0].astype(F32) + g2r[s, 1].astype(F32)) + (g2r[s, 2].astype(F32) + g2r[s, 3].astype(F32))
        total = total.reshape(4, 8, D)
        g3s[s] = jnp.concatenate([total[:, :, :HALF], total[:, :, HALF:]], axis=1).astype(BF16)
        z = zh * 4 + zl
        if s == 0:
            g3r[z] = g3s[s, zl]
        expect(g3r.at[pl.ds(0, 3 + s)], "P", 2, s)

        @pl.loop(1 - s, 4)
        def _(t):
            to = lax.rem(zl + t, 4)
            send(g3s.at[s, to], g3r.at[z], dev(halves[s], y, x, to, core), "P", 2, s)

    def weight_last():
        drain("r", "P", 2, 0)
        drain("r", "P", 2, 1)
        total = g3r[0].astype(F32)
        for i in range(1, 8):
            total = total + g3r[i].astype(F32)
        ow_ref[:, :HALF] = total[:8]
        ow_ref[:, HALF:] = total[8:]

    spread_cotangent(0)
    w_across(0)
    spread(0, 0)
    attend(0, 0)
    w_along(1)
    spread(0, 1)
    give_back(0, 0)
    w_across(1)
    spread_cotangent(1)
    attend(0, 1)
    spread(1, 0)
    give_back(0, 1)
    attend(1, 0)
    weight_first(0)
    spread(1, 1)
    give_back(1, 0)
    weight_second(0)
    attend(1, 1)
    weight_first(1)
    weight_third(0)
    weight_second(1)
    give_back(1, 1)
    weight_third(1)
    weight_last()
    for kept in keeps:
        kept.wait()
    for way, key in list(flight):
        drain(way, *key)


def place(*refs):
    sources, targets, sem = refs[:4], refs[4:8], refs[8]
    copies = [pltpu.make_async_copy(a, b, sem.at[i]) for i, (a, b) in enumerate(zip(sources, targets))]
    for copy in copies:
        copy.start()
    for copy in copies:
        copy.wait()


def on_device(queries, keys_saved, values_saved, grad_output, w_out):
    vmem = pl.BlockSpec(memory_space=pltpu.VMEM)
    dma = pltpu.SemaphoreType.DMA
    whole = jax.ShapeDtypeStruct(queries.shape, BF16)

    def buf(*shape):
        return pltpu.VMEM(shape, BF16)

    shapes = (whole, whole, whole, jax.ShapeDtypeStruct((8, D), F32))
    anywhere = pl.BlockSpec(memory_space=pl.ANY)
    results = pl.pallas_call(
        kernel,
        name="attention_backward",
        out_shape=shapes,
        in_specs=[anywhere] * 5,
        out_specs=(anywhere, anywhere, anywhere, vmem),
        scratch_shapes=[
            buf(*queries.shape), buf(*queries.shape), buf(*queries.shape), buf(*queries.shape), buf(*w_out.shape),
            buf(2, 2, 16, D),
            buf(3, 2, 2, 2, 16, HALF),
            buf(2, 4, 16, D),
            buf(2, 2, 16, 2, 16, 256),
            buf(2, 2, 16, 16, 256),
            buf(2, 16, 16, D),
            buf(2, 2, 16, 2, 16, 256),
            buf(2, 2, 16, 16, 256),
            buf(2, 4, 2, 32, D),
            buf(2, 2, 256, 256),
            buf(256, 512),
            buf(2, 2, 16, 3, 16, 256),
            buf(2, 2, 16, 3, 16, 256),
            buf(3, 2, 2, 2, 16, HALF),
            buf(3, 2, 2, 2, 16, HALF),
            buf(2, 2, 4, 32, D),
            buf(2, 4, 32, D),
            buf(2, 4, 32, D),
            buf(2, 4, 32, D),
            buf(2, 4, 16, HALF),
            buf(8, 16, HALF),
            dma((64,)), dma((64,)), dma((17,)),
        ],
        compiler_params=pltpu.CompilerParams(
            collective_id=0, has_side_effects=True, vmem_limit_bytes=56 * 1024 * 1024
        ),
        cost_estimate=pl.CostEstimate(flops=5 * 10**9, bytes_accessed=4 * 2**20, transcendentals=2**20),
    )(queries, keys_saved, values_saved, grad_output, w_out)
    return pl.pallas_call(
        place,
        name="place_results",
        out_shape=shapes,
        in_specs=[vmem] * 4,
        out_specs=(anywhere,) * 4,
        scratch_shapes=[dma((4,))],
        cost_estimate=pl.CostEstimate(flops=0, bytes_accessed=4 * 2**20, transcendentals=0),
    )(*results)


def solution(mesh):
    split = P("dp", "frame", None, None)
    return jax.shard_map(
        on_device,
        mesh=mesh,
        in_specs=(split, split, split, split, P("frame", None)),
        out_specs=(split, split, split, P(("frame", "dp"), None)),
        check_vma=False,
    )
```
